256 devices in a mesh: grp: 8 (over x, y_lo), ctx: 32 (over z, y_hi, core).
Axes of the slice: x: 4, y: 4 (y_hi: 2, y_lo: 2; y = y_hi * 2 + y_lo), z: 8, core: 2. Of those that a mesh axis runs over, the one named last changes fastest.
Arguments:
- inputs: bfloat16 [2, 32768, 8192], P(None, 'ctx'), may hold values from -6 to 6
- cotangent: bfloat16 [32768, 4096], P('ctx', 'grp'), may hold values from -0.029907227 to 0.029907227
- token_mask: int32 [32768], P('ctx'), may hold values 0 or 1
- block_owner: int32 [16, 8], replicated, may hold values from 0 to 7, as said below
- stat_left: float32 [8, 8192, 512], P('grp', 'ctx'), may hold values from -0.13 to 2.13
- stat_right: float32 [8, 8192, 512], P('grp', 'ctx'), may hold values from -0.13 to 2.13
- root_left: bfloat16 [8, 8192, 512], P('grp', 'ctx'), may hold values from -0.08 to 1.28
- root_right: bfloat16 [8, 8192, 512], P('grp', 'ctx'), may hold values from -0.08 to 1.28
Outputs:
- new_left: float32 [8, 8192, 512], P('grp', 'ctx')
- new_right: float32 [8, 8192, 512], P('grp', 'ctx')
- update: float32 [8, 8192, 512], P('grp', 'ctx')
The draws below stay inside these ranges and needn't reach their ends.
Inputs may be any that keep to these rules, and one draw needn't show every extreme that they name: Each row of block_owner is a rotation: block_owner[r, j] = (j + k) mod 8 with one k for each row r.
All inputs are finite; a program needn't handle non-finite values. No bound on the sum of `token_mask` on one device may be relied on, other than what follows from the above.
Results may differ from the reference program's by a relative error of at most 0.0003.
Values may be sent and summed in bfloat16 or wider, within the bound.
No kernel may reach another device: no remote copies, remote signals or barrier semaphores. Data moves between devices by JAX's collectives and lax.ppermute only.
A program may use at most 256 MiB of HBM per device.

```python
import jax
import jax.numpy as jnp
from jax import lax

BLK = 512
FEAT = 8192
ROWB = 16
COLS = 4096
TOKENS = 32768
N_GRP = 8


def symmetric_blocks(key, diag_low, diag_high, spread):
    first_key, second_key = jax.random.split(key)
    shape = (N_GRP, ROWB, BLK, BLK)
    noise = jax.random.uniform(first_key, shape, jnp.float32, -spread, spread)
    noise = (noise + jnp.swapaxes(noise, 2, 3)) * 0.7071
    diagonal = jax.random.uniform(second_key, (N_GRP, ROWB, BLK, 1), jnp.float32, diag_low, diag_high)
    identity = jnp.eye(BLK, dtype=jnp.float32)
    return (noise + diagonal * identity).reshape(N_GRP, FEAT, BLK)


def exact_root_blocks(key):
    first_key, second_key = jax.random.split(key)
    shape = (N_GRP, ROWB, BLK, BLK)
    steps = jax.random.randint(first_key, shape, -6, 7)
    steps = (steps + jnp.swapaxes(steps, 2, 3)).astype(jnp.float32) / 256.0
    levels = jax.random.randint(second_key, (N_GRP, ROWB, BLK, 1), 77, 154).astype(jnp.float32) / 128.0
    identity = jnp.eye(BLK, dtype=jnp.float32)
    return (steps * (1.0 - identity) + levels * identity).reshape(N_GRP, FEAT, BLK)


def draw_block_owner(key, part):
    key = jax.random.fold_in(key, 5)
    rotation = jax.random.randint(key, (ROWB, 1), 0, N_GRP)
    columns = jnp.arange(N_GRP, dtype=jnp.int32)[None, :]
    return ((rotation + columns) % N_GRP).astype(jnp.int32)


def draw_stat_left(key, part):
    key = jax.random.fold_in(key, 11)
    return symmetric_blocks(key, 1.0, 2.0, 0.09)


def draw_stat_right(key, part):
    key = jax.random.fold_in(key, 12)
    return symmetric_blocks(key, 1.0, 2.0, 0.09)


def draw_root_left(key, part):
    key = jax.random.fold_in(key, 13)
    return exact_root_blocks(key).astype(jnp.bfloat16)


def draw_root_right(key, part):
    key = jax.random.fold_in(key, 14)
    return exact_root_blocks(key).astype(jnp.bfloat16)


def set_ends(values, own_key, least, top_value):
    longest = values.shape.index(max(values.shape))
    spots = []
    for shift in (0, 1):
        where = [jax.random.randint(jax.random.fold_in(own_key, axis), (), 0, length) for axis, length in enumerate(values.shape)]
        where[longest] = (where[longest] + shift) % values.shape[longest]
        spots.append(tuple(where))
    return values.at[spots[0]].set(least).at[spots[1]].set(top_value)


def spiked(drawn, own_key, source, target, parts, factor):
    owner, partner = [(jnp.arange(drawn.shape[position]) // (drawn.shape[position] // parts)).reshape([-1 if axis == position else 1 for axis in range(drawn.ndim)]) for position in (source, target)]
    chosen = jax.random.permutation(own_key, parts)[partner]
    strong = (owner == chosen) | (owner == (partner + parts // 2) % parts)
    return jnp.where(strong, factor * drawn, drawn)


def shard_levels(own_key, dims, shards, least, largest):
    factor_of = 1.0
    for dim, parts in shards:
        draws = jax.random.uniform(jax.random.fold_in(jax.random.fold_in(own_key, 6), dim), (parts,), jnp.float32, least / len(shards), largest / len(shards))
        factor_of = factor_of * jnp.repeat(jnp.exp(draws), dims[dim] // parts).reshape((-1,) + (1,) * (len(dims) - 1 - dim))
    return factor_of


def centred(rng, shape, scale, limit, shards=(), kind=jnp.bfloat16):
    result = jax.random.normal(rng, shape, jnp.float32) * scale
    if len(shards) > 0:
        result = shard_levels(rng, shape, shards, -0.22, 0.18) * result
    return jnp.clip(result, min=-limit, max=limit).astype(kind)


def bell_draw_with(stream_key, dims, deviation, most, pieces, heavy, kind=jnp.bfloat16):
    result = deviation * jax.random.normal(stream_key, dims, jnp.float32)
    if pieces:
        result = result * shard_levels(stream_key, dims, pieces, -0.22, 0.18)
    return jnp.clip(spiked(result, jax.random.fold_in(stream_key, 3), *heavy), -most, most).astype(kind)


def setup_inputs(seed: int = 0) -> dict:
    arg_keys = jax.random.split(jax.random.key(seed), 9)
    inputs = bell_draw_with(arg_keys[0], (2, TOKENS, FEAT), 1.0, 6.0, ((1, 32),), (1, 2, 32, 2.75))
    cotangent = centred(arg_keys[1], (TOKENS, COLS), 0.004, 0.029907227, ((0, 32), (1, 8)))
    token_mask = set_ends((jax.random.randint(arg_keys[2], (TOKENS,), 0, 4) < 3).astype(jnp.int32), jax.random.fold_in(arg_keys[2], 1), 0, 1)
    block_owner = draw_block_owner(jax.random.fold_in(arg_keys[8], 71), 0)
    stat_left = draw_stat_left(jax.random.fold_in(arg_keys[8], 71), 0)
    stat_right = draw_stat_right(jax.random.fold_in(arg_keys[8], 71), 0)
    root_left = draw_root_left(jax.random.fold_in(arg_keys[8], 71), 0)
    root_right = draw_root_right(jax.random.fold_in(arg_keys[8], 71), 0)
    return dict(inputs=inputs, cotangent=cotangent, token_mask=token_mask, block_owner=block_owner, stat_left=stat_left, stat_right=stat_right, root_left=root_left, root_right=root_right)


decay_rate = 0.95


def to_slots(array):
    return array.reshape(N_GRP, ROWB, BLK, BLK).transpose(1, 0, 2, 3).astype(jnp.float32)


def from_slots(array):
    return array.transpose(1, 0, 2, 3).reshape(N_GRP, FEAT, BLK)


def reference(inputs, cotangent, token_mask, block_owner, stat_left, stat_right, root_left, root_right):
    masked = cotangent * token_mask[:, None].astype(jnp.bfloat16)
    split_at = COLS // 2
    first_part = jnp.dot(inputs[0].T, masked[:, :split_at], preferred_element_type=jnp.float32)
    second_part = jnp.dot(inputs[1].T, masked[:, split_at:], preferred_element_type=jnp.float32)
    gradient = jnp.concatenate([first_part, second_part], axis=1)
    blocks = gradient.reshape(ROWB, BLK, N_GRP, BLK).transpose(0, 2, 1, 3)
    slot_ids = jnp.arange(N_GRP, dtype=jnp.int32)
    matches = block_owner[:, None, :] == slot_ids[None, :, None]
    source_col = jnp.argmax(matches, axis=-1).astype(jnp.int32)
    slotted = jnp.take_along_axis(blocks, source_col[:, :, None, None], axis=1)
    highest = lax.Precision.HIGHEST
    left_term = jnp.einsum("rois,rojs->roij", slotted, slotted, precision=highest)
    right_term = jnp.einsum("rosi,rosj->roij", slotted, slotted, precision=highest)
    new_left = decay_rate * to_slots(stat_left) + (1.0 - decay_rate) * left_term
    new_right = decay_rate * to_slots(stat_right) + (1.0 - decay_rate) * right_term
    left_applied = jnp.einsum("rois,rosj->roij", to_slots(root_left), slotted, precision=highest)
    update = jnp.einsum("rois,rosj->roij", left_applied, to_slots(root_right), precision=highest)
    return from_slots(new_left), from_slots(new_right), from_slots(update)
```

```python
import functools

import jax
import jax.numpy as jnp
from jax import lax
from jax.experimental import pallas as pl
from jax.experimental.pallas import tpu as pltpu
from jax.sharding import PartitionSpec as P

decay_rate = 0.95
Z = 8
GROUPS = 8
UNIT = 256
BLOCK = 512
TAIL = 16
LEVELS = 32760.0
SMALLEST = 2.0**-100
MIB = 1 << 20
STAGES = ((4,), (3, -3), (2, -2, 1, -1, 0))


def place_of(offset):
    for stage, offsets in enumerate(STAGES):
        if offset in offsets:
            return stage, offsets.index(offset)


def rows_tile(rows):
    line = lax.broadcasted_iota(jnp.int32, (TAIL, UNIT), 0)
    tile = jnp.zeros((TAIL, UNIT), jnp.float32)
    for i, row in enumerate(rows):
        tile = jnp.where(line == i, row, tile)
    return tile.astype(jnp.int32).astype(jnp.int16)


def coded(value):
    top = jnp.maximum(jnp.max(jnp.abs(value), axis=0, keepdims=True), SMALLEST)
    code = jnp.ceil(jnp.log2(top) * 256.0)
    inverse = LEVELS / jnp.exp2(code * (1.0 / 256.0))
    return jnp.round(value * inverse).astype(jnp.int32).astype(jnp.int16), code


def scales(tile):
    code = tile.astype(jnp.int32).astype(jnp.float32)
    return jnp.exp2(code * (1.0 / 256.0)) * (1.0 / LEVELS)


def decoded(data, scale):
    return data.astype(jnp.int32).astype(jnp.float32) * scale


def write_message(ref, value):
    rows = value.shape[0]
    data, code = coded(value)
    ref[0:rows, :] = data
    ref[rows : rows + TAIL, :] = rows_tile([code])


def read_message(ref):
    rows = ref.shape[0] - TAIL
    return decoded(ref[0:rows, :], scales(ref[rows : rows + TAIL, :])[0:1])


def summed(keep, data, tail, half):
    return keep[0, 0] + decoded(data[0, 0], scales(tail[0, 0])[half : half + 1])


def partial_specs(pick):
    def spec(rows, row_index):
        return pl.BlockSpec(
            (1, 1, rows, UNIT), lambda *a: (*pick(a)[:2], row_index(pick(a)[2]), 0)
        )

    return [
        spec(UNIT, lambda half: half),
        spec(UNIT, lambda half: half),
        spec(TAIL, lambda half: BLOCK // TAIL),
    ]


def whole(shape):
    return pl.BlockSpec(shape, lambda *a: (0,) * len(shape))


def call(body, name, scalars, grid, in_specs, operands, out_specs, out_shape, flops=0, scratch=(), vmem=24):
    moved = sum(o.size * o.dtype.itemsize for o in out_shape)
    return pl.pallas_call(
        body,
        name=name,
        grid_spec=pltpu.PrefetchScalarGridSpec(
            num_scalar_prefetch=1,
            grid=grid,
            in_specs=in_specs,
            out_specs=out_specs,
            scratch_shapes=list(scratch),
        ),
        out_shape=out_shape,
        compiler_params=pltpu.CompilerParams(vmem_limit_bytes=vmem * MIB),
        cost_estimate=pl.CostEstimate(flops=flops, bytes_accessed=3 * moved, transcendentals=0),
    )(scalars, *operands)


def multiply_body(scalars, weights, sent_in, kept_in, keep_ref, sent_ref):
    partial = jnp.dot(weights[...], sent_in[0], preferred_element_type=jnp.float32)
    first, first_code = coded(partial[:UNIT])
    second, second_code = coded(partial[UNIT:])
    sent_ref[0, 0, 0:UNIT, :] = first
    sent_ref[0, 0, UNIT:BLOCK, :] = second
    sent_ref[0, 0, BLOCK : BLOCK + TAIL, :] = rows_tile([first_code, second_code])
    keep_ref[0, 0] = jnp.dot(weights[...], kept_in[0], preferred_element_type=jnp.float32)


def multiply(scalars, weights, inputs, offsets):
    count, tokens = len(offsets), inputs.shape[1]

    def spec(other):
        def index(t, y, s):
            core = 1 - s[2] if other else s[2]
            offset = jnp.int32(offsets[0])
            for i, o in enumerate(offsets[1:], 1):
                offset = jnp.where(t == i, o, offset)
            target = (s[1] + offset + Z) % Z
            return s[0], 0, (target * 2 + y) * 2 + core

        return pl.BlockSpec((1, tokens, UNIT), index)

    return call(
        multiply_body,
        "multiply",
        scalars,
        (count, 2),
        [whole((BLOCK, tokens)), spec(True), spec(False)],
        [weights, inputs, inputs],
        [
            pl.BlockSpec((1, 1, BLOCK, UNIT), lambda t, y, s: (t, y, 0, 0)),
            pl.BlockSpec((1, 1, BLOCK + TAIL, UNIT), lambda t, y, s: (t, y, 0, 0)),
        ],
        [
            jax.ShapeDtypeStruct((count, 2, BLOCK, UNIT), jnp.float32),
            jax.ShapeDtypeStruct((count, 2, BLOCK + TAIL, UNIT), jnp.int16),
        ],
        flops=count * 2 * 4 * BLOCK * tokens * UNIT,
    )


def across_body(scalars, keep, data, tail, out):
    write_message(out.at[0], summed(keep, data, tail, 1))


def across(scalars, part):
    keep, got = part
    count = keep.shape[0]
    return call(
        across_body,
        "across",
        scalars,
        (count,),
        partial_specs(lambda a: (a[0], 1 - a[1][3], 1)),
        [keep, got, got],
        [pl.BlockSpec((1, UNIT + TAIL, UNIT), lambda t, s: (t, 0, 0))],
        [jax.ShapeDtypeStruct((count, UNIT + TAIL, UNIT), jnp.int16)],
    )[0]


MESSAGE = jax.ShapeDtypeStruct((UNIT + TAIL, UNIT), jnp.int16)
HALF_MESSAGE = jax.ShapeDtypeStruct((UNIT // 2 + TAIL, UNIT), jnp.int16)


def along_body(scalars, *refs, count, arrived):
    step = 4 if arrived else 3
    ins, outs = refs[: step * count], refs[step * count :]
    for i in range(count):
        keep, data, tail = ins[i * step : i * step + 3]
        value = summed(keep, data, tail, 0)
        if arrived:
            value = value + read_message(ins[i * step + 3])
        write_message(outs[i], value)


def along(scalars, parts, members, received):
    specs, operands = [], []
    for i, (offset, half) in enumerate(members):
        stage, t = place_of(offset)
        keep, got = parts[stage]
        specs += partial_specs(lambda a, t=t, half=half: (t, half, 0))
        operands += [keep, got, got]
        if received is not None:
            specs.append(whole(MESSAGE.shape))
            operands.append(received[i])
    return call(
        functools.partial(along_body, count=len(members), arrived=received is not None),
        "along",
        scalars,
        (1,),
        specs,
        operands,
        [whole(MESSAGE.shape)] * len(members),
        [MESSAGE] * len(members),
    )


def second_first_body(scalars, keep, data, tail, crossed, up, down):
    value = summed(keep, data, tail, 1) + read_message(crossed.at[0])
    write_message(up, value[: UNIT // 2])
    write_message(down, value[UNIT // 2 :])


def crossed_spec(t):
    return pl.BlockSpec((1, UNIT + TAIL, UNIT), lambda *a: (t, 0, 0))


def own_half(t, half):
    return lambda a: (t, a[1][3], half)


def second_first(scalars, parts, crossed):
    stage, t = place_of(4)
    keep, got = parts[stage]
    return call(
        second_first_body,
        "second_first",
        scalars,
        (1,),
        partial_specs(own_half(t, 1)) + [crossed_spec(t)],
        [keep, got, got, crossed[stage]],
        [whole(HALF_MESSAGE.shape)] * 2,
        [HALF_MESSAGE] * 2,
    )


def second_body(scalars, *refs, halves):
    ins, outs = refs[:10], refs[10:]
    for i in range(2):
        keep, data, tail, crossed, arrived = ins[5 * i : 5 * i + 5]
        value = summed(keep, data, tail, 1) + read_message(crossed.at[0])
        more = read_message(arrived)
        if halves:
            upper, lower = value[: UNIT // 2], value[UNIT // 2 :]
            if i == 0:
                upper = upper + more
            else:
                lower = lower + more
            value = jnp.concatenate([upper, lower], 0)
        else:
            value = value + more
        write_message(outs[i], value)


def second(scalars, parts, crossed, distance, received):
    specs, operands = [], []
    for i, offset in enumerate((distance, -distance)):
        stage, t = place_of(offset)
        keep, got = parts[stage]
        specs += partial_specs(own_half(t, 1)) + [crossed_spec(t), whole(received[i].shape)]
        operands += [keep, got, got, crossed[stage], received[i]]
    return call(
        functools.partial(second_body, halves=distance == 3),
        "second",
        scalars,
        (1,),
        specs,
        operands,
        [whole(MESSAGE.shape)] * 2,
        [MESSAGE] * 2,
    )


def settle_body(scalars, *refs):
    ins, (sent, own) = refs[:10], refs[10:]
    values = []
    for half in range(2):
        keep, data, tail, up, down = ins[5 * half : 5 * half + 5]
        values.append(summed(keep, data, tail, 0) + read_message(up) + read_message(down))
    lower = scalars[3] == 0
    own[...] = jnp.where(lower, values[0], values[1])
    write_message(sent, jnp.where(lower, values[1], values[0]))


def settle(scalars, parts, received):
    stage, t = place_of(0)
    keep, got = parts[stage]
    specs, operands = [], []
    for half in range(2):
        specs += partial_specs(lambda a, half=half: (t, half, 0)) + [whole(MESSAGE.shape)] * 2
        operands += [keep, got, got, *received[half]]
    return call(
        settle_body,
        "settle",
        scalars,
        (1,),
        specs,
        operands,
        [whole(MESSAGE.shape), whole((UNIT, UNIT))],
        [MESSAGE, jax.ShapeDtypeStruct((UNIT, UNIT), jnp.float32)],
    )


def collect_body(scalars, own, over, keep, data, tail, crossed, up, down, out):
    first, first_code = coded(own[...] + read_message(over))
    value = summed(keep, data, tail, 1) + read_message(crossed.at[0])
    second_, second_code = coded(value + read_message(up) + read_message(down))
    out[0:UNIT, :] = first
    out[UNIT:BLOCK, :] = second_
    out[BLOCK : BLOCK + TAIL, :] = rows_tile([first_code, second_code])


def collect(scalars, own, over, parts, crossed, received):
    stage, t = place_of(0)
    keep, got = parts[stage]
    shape = (BLOCK + TAIL, UNIT)
    return call(
        collect_body,
        "collect",
        scalars,
        (1,),
        [whole((UNIT, UNIT)), whole(MESSAGE.shape), *partial_specs(own_half(t, 1)), crossed_spec(t)]
        + [whole(MESSAGE.shape)] * 2,
        [own, over, keep, got, got, crossed[stage], *received],
        [whole(shape)],
        [jax.ShapeDtypeStruct(shape, jnp.int16)],
    )[0]


def read_block(ref):
    scale = scales(ref[BLOCK : BLOCK + TAIL, :])
    return jnp.concatenate(
        [decoded(ref[0:UNIT, :], scale[0:1]), decoded(ref[UNIT:BLOCK, :], scale[1:2])], 0
    )


def product(a, b, contract):
    return lax.dot_general(a, b, (contract, ((), ())), preferred_element_type=jnp.float32)


def split(value):
    high = value.astype(jnp.bfloat16)
    return high, (value - high.astype(jnp.float32)).astype(jnp.bfloat16)


def finish_body(
    scalars, own_ref, other_ref, left_root, root_own, root_other, left_in, right_in,
    left_out, right_out, update_out, high, low, root,
):
    core = scalars[2]
    own_high, own_low = split(read_block(own_ref))
    other_high, other_low = split(read_block(other_ref))
    for c in range(2):
        mine, theirs = pl.ds(c * UNIT, UNIT), pl.ds((1 - c) * UNIT, UNIT)

        @pl.when(core == c)
        def _():
            high[:, mine] = own_high
            low[:, mine] = own_low
            high[:, theirs] = other_high
            low[:, theirs] = other_low
            root[mine, :] = root_own[0]
            root[theirs, :] = root_other[...]

    rate = 1.0 - decay_rate
    full_high, full_low = high[...], low[...]
    by_rows = ((0,), (0,))
    by_columns = ((1,), (1,))
    term = product(own_high, full_high, by_rows)
    term += product(own_high, full_low, by_rows) + product(own_low, full_high, by_rows)
    left_out[0] = decay_rate * left_in[0] + rate * term
    here = pl.ds(pl.multiple_of(core * UNIT, UNIT), UNIT)
    term = product(high[here, :], full_high, by_columns)
    term += product(high[here, :], full_low, by_columns)
    term += product(low[here, :], full_high, by_columns)
    right_out[0] = decay_rate * right_in[0] + rate * term
    applied = product(left_root[0], full_high, by_columns)
    applied += product(left_root[0], full_low, by_columns)
    applied_high, applied_low = split(applied)
    plain = ((1,), (0,))
    update_out[0] = product(applied_high, root[...], plain) + product(applied_low, root[...], plain)


def finish(scalars, own, other, left_root, root_own, root_other, left_in, right_in):
    result = jax.ShapeDtypeStruct((1, UNIT, BLOCK), jnp.float32)
    operands = [own, other, left_root, root_own, root_other, left_in, right_in]
    return call(
        finish_body,
        "finish",
        scalars,
        (1,),
        [whole(o.shape) for o in operands],
        operands,
        [whole(result.shape)] * 3,
        [result] * 3,
        flops=20 * UNIT * BLOCK * BLOCK,
        scratch=[
            pltpu.VMEM((BLOCK, BLOCK), jnp.bfloat16),
            pltpu.VMEM((BLOCK, BLOCK), jnp.bfloat16),
            pltpu.VMEM((BLOCK, BLOCK), jnp.bfloat16),
        ],
    )


def per_device(
    inputs, cotangent, token_mask, block_owner, stat_left, stat_right, root_left, root_right
):
    own_group = lax.axis_index("grp")
    position = lax.axis_index("ctx")
    count = 4 * Z

    def to_core(value):
        return lax.ppermute(value, "ctx", [(i, i ^ 1) for i in range(count)])

    def over_y(value):
        return lax.ppermute(value, "ctx", [(i, i ^ 2) for i in range(count)])

    def up_z(value):
        return lax.ppermute(value, "ctx", [(i, (i + 4) % count) for i in range(count)])

    def down_z(value):
        return lax.ppermute(value, "ctx", [(i, (i - 4) % count) for i in range(count)])

    scalars = jnp.stack(
        [own_group // (GROUPS // 2), position // 4, position % 2, position // 2 % 2]
    ).astype(jnp.int32)
    weights = (cotangent * token_mask[:, None].astype(jnp.bfloat16)).T
    parts, crossed = [], []
    for offsets in STAGES:
        keep, sent = multiply(scalars, weights, inputs, offsets)
        parts.append((keep, to_core(sent)))
        crossed.append(over_y(across(scalars, parts[-1])))
    root_other = to_core(root_right[0])

    up_far, down_far = along(scalars, parts, ((4, 0), (4, 1)), None)
    late = [up_z(up_far), down_z(down_far)]
    down_near, up_near = along(scalars, parts, ((-3, 0), (3, 1)), None)
    early = [down_z(down_near), up_z(up_near)]
    halves = second_first(scalars, parts, crossed)
    across_both = [up_z(halves[0]), down_z(halves[1])]
    for distance in (3, 2, 1):
        up, down = along(scalars, parts, ((distance, 0), (-distance, 1)), late)
        late = [up_z(up), down_z(down)]
        if distance < 3:
            down, up = along(scalars, parts, ((-distance, 0), (distance, 1)), early)
            early = [down_z(down), up_z(up)]
        up, down = second(scalars, parts, crossed, distance, across_both)
        across_both = [up_z(up), down_z(down)]
    sent, own = settle(scalars, parts, ((late[0], early[0]), (early[1], late[1])))
    block = collect(scalars, own, over_y(sent), parts, crossed, across_both)

    rotation = lax.dynamic_index_in_dim(block_owner[:, 0], position // 2, 0, keepdims=False)

    def rotated(steps):
        if steps == 0:
            return lambda value: value
        pairs = [(source, (source + steps) % GROUPS) for source in range(GROUPS)]
        return lambda value: lax.ppermute(value, "grp", pairs)

    block = lax.switch(rotation, [rotated(steps) for steps in range(GROUPS)], block)
    return tuple(
        finish(
            scalars, block, to_core(block), root_left, root_right, root_other, stat_left, stat_right
        )
    )


def solution(mesh):
    in_specs = (
        P(None, "ctx", None),
        P("ctx", "grp"),
        P("ctx"),
        P(),
        P("grp", "ctx", None),
        P("grp", "ctx", None),
        P("grp", "ctx", None),
        P("grp", "ctx", None),
    )
    out_specs = (P("grp", "ctx", None), P("grp", "ctx", None), P("grp", "ctx", None))
    return jax.shard_map(
        per_device, mesh=mesh, in_specs=in_specs, out_specs=out_specs, check_vma=False
    )
```

```python
import functools

import jax
import jax.numpy as jnp
from jax import lax
from jax.experimental import pallas as pl
from jax.experimental.pallas import tpu as pltpu
from jax.sharding import PartitionSpec as P

decay_rate = 0.95
Z = 8
GROUPS = 8
UNIT = 256
BLOCK = 512
TAIL = 16
LEVELS = 32760.0
SMALLEST = 2.0**-100
MIB = 1 << 20
HALF = UNIT
LANES = 4 * UNIT
ORDER = ("m4", "m3", "a4", "m2", "y4", "y3", "a3", "m1", "b4", "a2", "y2", "b3", "m0", "a1", "y1", "b2", "y0", "ax", "b1")
COSTS = {4: 30000000000, 3: 60000000000, 2: 60000000000, 1: 60000000000, 0: 30000000000}
HOP_COST = 3000000000


def rows_tile(rows):
    shape = (TAIL, rows[0].shape[1])
    line = lax.broadcasted_iota(jnp.int32, shape, 0)
    tile = jnp.zeros(shape, jnp.float32)
    for i, row in enumerate(rows):
        tile = jnp.where(line == i, row, tile)
    return tile.astype(jnp.int32).astype(jnp.int16)


def coded(value):
    top = jnp.maximum(jnp.max(jnp.abs(value), axis=0, keepdims=True), SMALLEST)
    code = jnp.ceil(jnp.log2(top) * 256.0)
    inverse = LEVELS / jnp.exp2(code * (1.0 / 256.0))
    return jnp.round(value * inverse).astype(jnp.int32).astype(jnp.int16), code


def scales(tile):
    code = tile.astype(jnp.int32).astype(jnp.float32)
    return jnp.exp2(code * (1.0 / 256.0)) * (1.0 / LEVELS)


def decoded(data, scale):
    return data.astype(jnp.int32).astype(jnp.float32) * scale


def message(value):
    data, code = coded(value)
    return jnp.concatenate([data, rows_tile([code])], 0)


def opened(value):
    return decoded(value[:HALF], scales(value[HALF:])[0:1])


def whole(shape):
    return pl.BlockSpec(shape, lambda *a: (0,) * len(shape))


def wire(lanes):
    return jax.ShapeDtypeStruct((HALF + TAIL, lanes), jnp.int16)


def plain(lanes):
    return jax.ShapeDtypeStruct((HALF, lanes), jnp.float32)


def call(body, name, scalars, grid, in_specs, operands, out_specs, out_shape, after=(), moved=1024, flops=HOP_COST, scratch=()):
    count = len(operands)

    def ordered(scalar_refs, *refs):
        body(scalar_refs, *refs[:count], *refs[count + len(after) :])

    return pl.pallas_call(
        ordered,
        name=name,
        grid_spec=pltpu.PrefetchScalarGridSpec(
            num_scalar_prefetch=1,
            grid=grid,
            in_specs=list(in_specs) + [pl.BlockSpec(memory_space=pl.ANY)] * len(after),
            out_specs=out_specs,
            scratch_shapes=list(scratch),
        ),
        out_shape=out_shape,
        compiler_params=pltpu.CompilerParams(vmem_limit_bytes=24 * MIB),
        cost_estimate=pl.CostEstimate(flops=flops, bytes_accessed=moved, transcendentals=0),
    )(scalars, *operands, *after)


def pick(condition, first, second):
    return jnp.where(condition, first, second), jnp.where(condition, second, first)


def by_core(left, right, is_first):
    lower = jnp.concatenate([left[:, :UNIT], right[:, :UNIT]], 1)
    upper = jnp.concatenate([left[:, UNIT:], right[:, UNIT:]], 1)
    return pick(is_first, lower, upper)


def multiply_body(scalars, weights, sent_in, kept_in, keep_ref, sent_ref):
    contract = ((0,), (0,))
    partial = product(weights[...], sent_in[0], contract)
    for half in range(2):
        sent_ref[half] = message(partial[half * HALF : (half + 1) * HALF])
    keep_ref[...] = product(weights[...], kept_in[0], contract)


def end_body(scalars, weights, left_in, right_in, keep_ref, sent_ref, *, whole_rows):
    contract = ((0,), (0,))
    left = product(weights[...], left_in[0], contract)
    right = product(weights[...], right_in[0], contract)
    is_first = scalars[2] == 0
    if whole_rows:
        kept, sent = pick(is_first, left[:HALF], right[:HALF])
    else:
        kept, sent = by_core(left[:HALF], right[:HALF], is_first)
    keep_ref[:HALF] = kept
    sent_ref[0] = message(sent)
    kept, sent = by_core(left[HALF:], right[HALF:], is_first)
    keep_ref[HALF:] = kept
    sent_ref[1] = message(sent)


def multiply(scalars, weights, inputs, distance, after):
    tokens = inputs.shape[1]
    width = BLOCK
    at_end = distance in (0, Z // 2)

    def spec(way):
        def index(j, s):
            if at_end:
                return s[0], 0, (s[1] + distance) % Z * 2 + way
            sign = 2 * way - 1
            target = (s[1] + sign * (1 - 2 * s[2]) * distance + Z) % Z
            return s[0], 0, target * 2 + j

        return pl.BlockSpec((1, tokens, width), index)

    lanes = LANES // 2 if at_end else LANES
    body = multiply_body
    if at_end:
        body = functools.partial(end_body, whole_rows=distance > 0)
    return call(
        body,
        "multiply",
        scalars,
        (lanes // width,),
        [whole((tokens, BLOCK)), spec(0), spec(1)],
        [weights, inputs, inputs],
        [
            pl.BlockSpec((BLOCK, width), lambda j, s: (0, j)),
            pl.BlockSpec((2, HALF + TAIL, width), lambda j, s: (0, 0, j)),
        ],
        [
            jax.ShapeDtypeStruct((BLOCK, lanes), jnp.float32),
            jax.ShapeDtypeStruct((2, HALF + TAIL, lanes), jnp.int16),
        ],
        after=after,
        flops=COSTS[distance],
    )


def part_specs(half, lanes, place):
    return [
        pl.BlockSpec((HALF, lanes), lambda i, s: (half, place(s))),
        pl.BlockSpec((1, HALF + TAIL, lanes), lambda i, s: (half, 0, place(s))),
    ]


def first_place(s):
    return 0


def own_place(s):
    return s[3]


def other_place(s):
    return 1 - s[3]


def hop_body(scalars, keep, got, *refs, count, outs):
    value = keep[...] + opened(got[0])
    for ref in refs[:count]:
        more = opened(ref[...])
        if more.shape[1] < value.shape[1]:
            nothing = jnp.zeros_like(more)
            lower, upper = jnp.concatenate([more, nothing], 1), jnp.concatenate([nothing, more], 1)
            more = jnp.where(scalars[2] == 0, lower, upper)
        value = value + more
    if outs == 1:
        refs[-1][...] = message(value)
        return
    is_first = scalars[2] == 0
    half = value.shape[1] // 2
    if half == UNIT:
        own, other = pick(is_first, value[:, :UNIT], value[:, UNIT:])
    else:
        own, other = by_core(value[:, :half], value[:, half:], is_first)
    refs[-2][...] = message(own)
    refs[-1][...] = message(other)


def hop(name, scalars, part, half, lanes, place, adds, outs, after):
    keep, got = part
    shape = wire(lanes // outs)
    return call(
        functools.partial(hop_body, count=len(adds), outs=outs),
        name,
        scalars,
        (1,),
        part_specs(half, lanes, place) + [whole(o.shape) for o in adds],
        [keep, got] + adds,
        [whole(shape.shape)] * outs,
        [shape] * outs,
        after=after,
    )


def cross_body(scalars, keep, got, up, down, sent, kept):
    value = keep[...] + opened(got[0]) + opened(up[...]) + opened(down[...])
    kept[...], other = pick(scalars[3] == 0, value[:, :UNIT], value[:, UNIT:])
    sent[...] = message(other)


def cross(name, scalars, part, adds, after):
    keep, got = part
    return call(
        cross_body,
        name,
        scalars,
        (1,),
        part_specs(0, 2 * UNIT, first_place) + [whole(o.shape) for o in adds],
        [keep, got] + adds,
        [whole(wire(UNIT).shape), whole((HALF, UNIT))],
        [wire(UNIT), plain(UNIT)],
        after=after,
    )


def collect_body(scalars, own, over, keep, got, crossed, up, down, out):
    first, first_code = coded(own[...] + opened(over[...]))
    value = keep[...] + opened(got[0]) + opened(crossed[...])
    second, second_code = coded(value + opened(up[...]) + opened(down[...]))
    out[0:UNIT, :] = first
    out[UNIT:BLOCK, :] = second
    out[BLOCK : BLOCK + TAIL, :] = rows_tile([first_code, second_code])


def collect(scalars, own, over, part, adds):
    shape = (BLOCK + TAIL, UNIT)
    keep, got = part
    return call(
        collect_body,
        "collect",
        scalars,
        (1,),
        [whole(own.shape), whole(over.shape)]
        + part_specs(1, UNIT, own_place)
        + [whole(o.shape) for o in adds],
        [own, over, keep, got] + adds,
        [whole(shape)],
        [jax.ShapeDtypeStruct(shape, jnp.int16)],
    )[0]


def read_block(ref):
    scale = scales(ref[BLOCK : BLOCK + TAIL, :])
    return jnp.concatenate(
        [decoded(ref[0:UNIT, :], scale[0:1]), decoded(ref[UNIT:BLOCK, :], scale[1:2])], 0
    )


def product(a, b, contract):
    return lax.dot_general(a, b, (contract, ((), ())), preferred_element_type=jnp.float32)


def split(value):
    high = value.astype(jnp.bfloat16)
    return high, (value - high.astype(jnp.float32)).astype(jnp.bfloat16)


def finish_body(
    scalars, own_ref, other_ref, left_root, root_own, root_other, left_in, right_in,
    left_out, right_out, update_out, high, low, root,
):
    core = scalars[2]
    own_high, own_low = split(read_block(own_ref))
    other_high, other_low = split(read_block(other_ref))
    for c in range(2):
        mine, theirs = pl.ds(c * UNIT, UNIT), pl.ds((1 - c) * UNIT, UNIT)

        @pl.when(core == c)
        def _():
            high[:, mine] = own_high
            low[:, mine] = own_low
            high[:, theirs] = other_high
            low[:, theirs] = other_low
            root[mine, :] = root_own[0]
            root[theirs, :] = root_other[...]

    rate = 1.0 - decay_rate
    full_high, full_low = high[...], low[...]
    by_rows = ((0,), (0,))
    by_columns = ((1,), (1,))
    term = product(own_high, full_high, by_rows)
    term += product(own_high, full_low, by_rows) + product(own_low, full_high, by_rows)
    left_out[0] = decay_rate * left_in[0] + rate * term
    here = pl.ds(pl.multiple_of(core * UNIT, UNIT), UNIT)
    term = product(high[here, :], full_high, by_columns)
    term += product(high[here, :], full_low, by_columns)
    term += product(low[here, :], full_high, by_columns)
    right_out[0] = decay_rate * right_in[0] + rate * term
    applied = product(left_root[0], full_high, by_columns)
    applied += product(left_root[0], full_low, by_columns)
    applied_high, applied_low = split(applied)
    plain = ((1,), (0,))
    update_out[0] = product(applied_high, root[...], plain) + product(applied_low, root[...], plain)


def finish(scalars, own, other, left_root, root_own, root_other, left_in, right_in):
    result = jax.ShapeDtypeStruct((1, UNIT, BLOCK), jnp.float32)
    operands = [own, other, left_root, root_own, root_other, left_in, right_in]
    return call(
        finish_body,
        "finish",
        scalars,
        (1,),
        [whole(o.shape) for o in operands],
        operands,
        [whole(result.shape)] * 3,
        [result] * 3,
        flops=20 * UNIT * BLOCK * BLOCK,
        scratch=[
            pltpu.VMEM((BLOCK, BLOCK), jnp.bfloat16),
            pltpu.VMEM((BLOCK, BLOCK), jnp.bfloat16),
            pltpu.VMEM((BLOCK, BLOCK), jnp.bfloat16),
        ],
    )


def per_device(
    inputs, cotangent, token_mask, block_owner, stat_left, stat_right, root_left, root_right
):
    own_group = lax.axis_index("grp")
    position = lax.axis_index("ctx")
    count = 4 * Z

    def to_core(value):
        return lax.ppermute(value, "ctx", [(i, i ^ 1) for i in range(count)])

    def over_y(value):
        return lax.ppermute(value, "ctx", [(i, i ^ 2) for i in range(count)])

    def along_z(value, swap=0):
        pairs = [(i, (i + (4 if i % 2 == 0 else -4)) % count ^ swap) for i in range(count)]
        return lax.ppermute(value, "ctx", pairs)

    scalars = jnp.stack(
        [own_group // (GROUPS // 2), position // 4, position % 2, position // 2 % 2]
    ).astype(jnp.int32)
    masked = cotangent * token_mask[:, None].astype(jnp.bfloat16)
    root_other = to_core(root_right[0])
    parts, arrived, crossed = {}, {}, {}
    last = []
    for token in ORDER:
        name, step = token[0], token[1]
        if name == "m":
            distance = int(step)
            if distance == 3:
                last.append(root_other)
            keep, sent = multiply(scalars, masked, inputs, distance, last)
            last = [keep]
            parts[distance] = keep, to_core(sent)
        elif step == "x":
            sent, own = cross(token, scalars, parts[0], arrived["a"], last)
            last = [own]
            crossed["a"] = own, over_y(sent)
        else:
            distance = int(step)
            lanes = parts[distance][0].shape[1]
            outs = 2 if distance == 1 and name != "y" else 1
            adds = list(arrived.get(name, []))
            place = first_place
            if name != "a":
                lanes //= 2
                place = own_place
            if name == "b":
                adds.insert(0, crossed[distance])
            elif name == "y":
                place = other_place
            half = 0 if name == "a" else 1
            made = hop(token, scalars, parts[distance], half, lanes, place, adds, outs, last)
            last = [made[-1]]
            if name == "y":
                crossed[distance] = over_y(made[0])
            else:
                arrived[name] = [along_z(value, swap) for swap, value in enumerate(made)]
    block = collect(scalars, *crossed["a"], parts[0], [crossed[0]] + arrived["b"])

    rotation = lax.dynamic_index_in_dim(block_owner[:, 0], position // 2, 0, keepdims=False)

    def rotated(steps):
        if steps == 0:
            return lambda value: value
        pairs = [(source, (source + steps) % GROUPS) for source in range(GROUPS)]
        return lambda value: lax.ppermute(value, "grp", pairs)

    block = lax.switch(rotation, [rotated(steps) for steps in range(GROUPS)], block)
    return tuple(
        finish(
            scalars, block, to_core(block), root_left, root_right, root_other, stat_left, stat_right
        )
    )


def solution(mesh):
    in_specs = (
        P(None, "ctx", None),
        P("ctx", "grp"),
        P("ctx"),
        P(),
        P("grp", "ctx", None),
        P("grp", "ctx", None),
        P("grp", "ctx", None),
        P("grp", "ctx", None),
    )
    out_specs = (P("grp", "ctx", None), P("grp", "ctx", None), P("grp", "ctx", None))
    return jax.shard_map(
        per_device, mesh=mesh, in_specs=in_specs, out_specs=out_specs, check_vma=False
    )
```

```python
import functools

import jax
import jax.numpy as jnp
from jax import lax
from jax.experimental import pallas as pl
from jax.experimental.pallas import tpu as pltpu
from jax.sharding import PartitionSpec as P

decay_rate = 0.95
Z = 8
GROUPS = 8
UNIT = 256
BLOCK = 512
TAIL = 16
LEVELS = 32760.0
SMALLEST = 2.0**-100
MIB = 1 << 20
HALF = UNIT
LANES = 4 * UNIT
ORDER = ("m4", "m3", "a4", "m2", "y34", "a3", "m1", "m0", "b4", "a2", "y2", "b3", "y1", "a1", "b2", "y0", "ax", "b1")
COSTS = {4: 10000000000, 3: 20000000000, 2: 20000000000, 1: 20000000000, 0: 10000000000}
HOP_COST = 3000000000


def rows_tile(rows):
    shape = (TAIL, rows[0].shape[1])
    line = lax.broadcasted_iota(jnp.int32, shape, 0)
    tile = jnp.zeros(shape, jnp.float32)
    for i, row in enumerate(rows):
        tile = jnp.where(line == i, row, tile)
    return tile.astype(jnp.int32).astype(jnp.int16)


def coded(value):
    top = jnp.maximum(jnp.max(jnp.abs(value), axis=0, keepdims=True), SMALLEST)
    code = jnp.ceil(jnp.log2(top) * 256.0)
    inverse = LEVELS / jnp.exp2(code * (1.0 / 256.0))
    return jnp.round(value * inverse).astype(jnp.int32).astype(jnp.int16), code


def scales(tile):
    code = tile.astype(jnp.int32).astype(jnp.float32)
    return jnp.exp2(code * (1.0 / 256.0)) * (1.0 / LEVELS)


def decoded(data, scale):
    return data.astype(jnp.int32).astype(jnp.float32) * scale


def message(value):
    data, code = coded(value)
    return jnp.concatenate([data, rows_tile([code])], 0)


def opened(value):
    return decoded(value[:HALF], scales(value[HALF:])[0:1])


def whole(shape):
    return pl.BlockSpec(shape, lambda *a: (0,) * len(shape))


def wire(lanes):
    return jax.ShapeDtypeStruct((HALF + TAIL, lanes), jnp.int16)


def plain(lanes):
    return jax.ShapeDtypeStruct((HALF, lanes), jnp.float32)


def call(body, name, scalars, grid, in_specs, operands, out_specs, out_shape, after=(), moved=1024, flops=HOP_COST, scratch=(), vmem=24):
    count = len(operands)

    def ordered(scalar_refs, *refs):
        body(scalar_refs, *refs[:count], *refs[count + len(after) :])

    return pl.pallas_call(
        ordered,
        name=name,
        grid_spec=pltpu.PrefetchScalarGridSpec(
            num_scalar_prefetch=1,
            grid=grid,
            in_specs=list(in_specs) + [pl.BlockSpec(memory_space=pl.ANY)] * len(after),
            out_specs=out_specs,
            scratch_shapes=list(scratch),
        ),
        out_shape=out_shape,
        compiler_params=pltpu.CompilerParams(vmem_limit_bytes=vmem * MIB),
        cost_estimate=pl.CostEstimate(flops=flops, bytes_accessed=moved, transcendentals=0),
    )(scalars, *operands, *after)


def pick(condition, first, second):
    return jnp.where(condition, first, second), jnp.where(condition, second, first)


def by_core(left, right, is_first):
    lower = jnp.concatenate([left[:, :UNIT], right[:, :UNIT]], 1)
    upper = jnp.concatenate([left[:, UNIT:], right[:, UNIT:]], 1)
    return pick(is_first, lower, upper)


def multiply_body(scalars, weights, sent_in, kept_in, keep_ref, sent_ref):
    contract = ((0,), (0,))
    partial = product(weights[...], sent_in[0], contract)
    for half in range(2):
        sent_ref[half] = message(partial[half * HALF : (half + 1) * HALF])
    keep_ref[...] = product(weights[...], kept_in[0], contract)


def end_body(scalars, weights, *refs, masking):
    if masking:
        mask_ref, left_in, right_in, keep_ref, sent_ref, masked_ref = refs
        rows = jnp.broadcast_to(mask_ref[...].astype(jnp.float32), (8, mask_ref.shape[1]))
        column = rows.T[:, 0:1].astype(jnp.bfloat16)
        masked_ref[...] = weights[...] * column
        weights = masked_ref
    else:
        left_in, right_in, keep_ref, sent_ref = refs
    contract = ((0,), (0,))
    left = product(weights[...], left_in[0], contract)
    right = product(weights[...], right_in[0], contract)
    is_first = scalars[2] == 0
    if masking:
        kept, sent = pick(is_first, left[:HALF], right[:HALF])
    else:
        kept, sent = by_core(left[:HALF], right[:HALF], is_first)
    keep_ref[:HALF] = kept
    sent_ref[0] = message(sent)
    kept, sent = by_core(left[HALF:], right[HALF:], is_first)
    keep_ref[HALF:] = kept
    sent_ref[1] = message(sent)


def multiply(scalars, weights, inputs, distance, after):
    tokens = inputs.shape[1]
    width = BLOCK
    at_end = distance in (0, Z // 2)

    def spec(way):
        def index(j, s):
            if at_end:
                return s[0], 0, (s[1] + distance) % Z * 2 + way
            sign = 2 * way - 1
            target = (s[1] + sign * (1 - 2 * s[2]) * distance + Z) % Z
            return s[0], 0, target * 2 + j

        return pl.BlockSpec((1, tokens, width), index)

    lanes = LANES // 2 if at_end else LANES
    masking = distance == Z // 2
    body = functools.partial(end_body, masking=masking) if at_end else multiply_body
    first = list(weights) if masking else [weights]
    more = [jax.ShapeDtypeStruct((tokens, BLOCK), jnp.bfloat16)] if masking else []
    return call(
        body,
        "multiply",
        scalars,
        (lanes // width,),
        [whole(o.shape) for o in first] + [spec(0), spec(1)],
        first + [inputs, inputs],
        [
            pl.BlockSpec((BLOCK, width), lambda j, s: (0, j)),
            pl.BlockSpec((2, HALF + TAIL, width), lambda j, s: (0, 0, j)),
        ]
        + [whole(o.shape) for o in more],
        [
            jax.ShapeDtypeStruct((BLOCK, lanes), jnp.float32),
            jax.ShapeDtypeStruct((2, HALF + TAIL, lanes), jnp.int16),
        ]
        + more,
        after=after,
        flops=COSTS[distance],
        vmem=24,
    )


def part_specs(half, lanes, place):
    return [
        pl.BlockSpec((HALF, lanes), lambda i, s: (half, place(s))),
        pl.BlockSpec((1, HALF + TAIL, lanes), lambda i, s: (half, 0, place(s))),
    ]


def first_place(s):
    return 0


def own_place(s):
    return s[3]


def other_place(s):
    return 1 - s[3]


def hop_body(scalars, keep, got, *refs, count, outs):
    value = keep[...] + opened(got[0])
    for ref in refs[:count]:
        more = opened(ref[...])
        if more.shape[1] < value.shape[1]:
            nothing = jnp.zeros_like(more)
            lower, upper = jnp.concatenate([more, nothing], 1), jnp.concatenate([nothing, more], 1)
            more = jnp.where(scalars[2] == 0, lower, upper)
        value = value + more
    if outs == 1:
        refs[-1][...] = message(value)
        return
    is_first = scalars[2] == 0
    half = value.shape[1] // 2
    if half == UNIT:
        own, other = pick(is_first, value[:, :UNIT], value[:, UNIT:])
    else:
        own, other = by_core(value[:, :half], value[:, half:], is_first)
    refs[-2][...] = message(own)
    refs[-1][...] = message(other)


def hop(name, scalars, part, half, lanes, place, adds, outs, after):
    keep, got = part
    shape = wire(lanes // outs)
    return call(
        functools.partial(hop_body, count=len(adds), outs=outs),
        name,
        scalars,
        (1,),
        part_specs(half, lanes, place) + [spec for _, spec in adds],
        [keep, got] + [value for value, _ in adds],
        [whole(shape.shape)] * outs,
        [shape] * outs,
        after=after,
    )


def across_body(scalars, *refs):
    out, start = refs[-1], 0
    for keep, got in zip(refs[:-1:2], refs[1:-1:2]):
        value = keep[...] + opened(got[0])
        lanes = value.shape[1]
        out[:, start : start + lanes] = message(value)
        start += lanes


def across(name, scalars, chosen, after):
    specs, operands, total = [], [], 0
    for keep, got in chosen:
        lanes = keep.shape[1] // 2
        specs += part_specs(1, lanes, other_place)
        operands += [keep, got]
        total += lanes
    shape = wire(total)
    return call(
        across_body,
        name,
        scalars,
        (1,),
        specs,
        operands,
        [whole(shape.shape)],
        [shape],
        after=after,
    )[0]


def cross_body(scalars, keep, got, up, down, sent, kept):
    value = keep[...] + opened(got[0]) + opened(up[...]) + opened(down[...])
    kept[...], other = pick(scalars[3] == 0, value[:, :UNIT], value[:, UNIT:])
    sent[...] = message(other)


def cross(name, scalars, part, adds, after):
    keep, got = part
    return call(
        cross_body,
        name,
        scalars,
        (1,),
        part_specs(0, 2 * UNIT, first_place) + [whole(o.shape) for o in adds],
        [keep, got] + adds,
        [whole(wire(UNIT).shape), whole((HALF, UNIT))],
        [wire(UNIT), plain(UNIT)],
        after=after,
    )


def collect_body(scalars, own, over, keep, got, crossed, up, down, out):
    first, first_code = coded(own[...] + opened(over[...]))
    value = keep[...] + opened(got[0]) + opened(crossed[...])
    second, second_code = coded(value + opened(up[...]) + opened(down[...]))
    out[0:UNIT, :] = first
    out[UNIT:BLOCK, :] = second
    out[BLOCK : BLOCK + TAIL, :] = rows_tile([first_code, second_code])


def collect(scalars, own, over, part, adds):
    shape = (BLOCK + TAIL, UNIT)
    keep, got = part
    return call(
        collect_body,
        "collect",
        scalars,
        (1,),
        [whole(own.shape), whole(over.shape)]
        + part_specs(1, UNIT, own_place)
        + [whole(o.shape) for o in adds],
        [own, over, keep, got] + adds,
        [whole(shape)],
        [jax.ShapeDtypeStruct(shape, jnp.int16)],
    )[0]


def read_block(ref):
    scale = scales(ref[BLOCK : BLOCK + TAIL, :])
    return jnp.concatenate(
        [decoded(ref[0:UNIT, :], scale[0:1]), decoded(ref[UNIT:BLOCK, :], scale[1:2])], 0
    )


def product(a, b, contract):
    return lax.dot_general(a, b, (contract, ((), ())), preferred_element_type=jnp.float32)


def split(value):
    high = value.astype(jnp.bfloat16)
    return high, (value - high.astype(jnp.float32)).astype(jnp.bfloat16)


def finish_body(
    scalars, own_ref, other_ref, left_root, root_own, root_other, left_in, right_in,
    left_out, right_out, update_out, high, low, root,
):
    core = scalars[2]
    own_high, own_low = split(read_block(own_ref))
    other_high, other_low = split(read_block(other_ref))
    for c in range(2):
        mine, theirs = pl.ds(c * UNIT, UNIT), pl.ds((1 - c) * UNIT, UNIT)

        @pl.when(core == c)
        def _():
            high[:, mine] = own_high
            low[:, mine] = own_low
            high[:, theirs] = other_high
            low[:, theirs] = other_low
            root[mine, :] = root_own[0]
            root[theirs, :] = root_other[...]

    rate = 1.0 - decay_rate
    full_high, full_low = high[...], low[...]
    by_rows = ((0,), (0,))
    by_columns = ((1,), (1,))
    term = product(own_high, full_high, by_rows)
    term += product(own_high, full_low, by_rows) + product(own_low, full_high, by_rows)
    left_out[0] = decay_rate * left_in[0] + rate * term
    here = pl.ds(pl.multiple_of(core * UNIT, UNIT), UNIT)
    term = product(high[here, :], full_high, by_columns)
    term += product(high[here, :], full_low, by_columns)
    term += product(low[here, :], full_high, by_columns)
    right_out[0] = decay_rate * right_in[0] + rate * term
    applied = product(left_root[0], full_high, by_columns)
    applied += product(left_root[0], full_low, by_columns)
    applied_high, applied_low = split(applied)
    plain = ((1,), (0,))
    update_out[0] = product(applied_high, root[...], plain) + product(applied_low, root[...], plain)


def finish(scalars, own, other, left_root, root_own, root_other, left_in, right_in):
    result = jax.ShapeDtypeStruct((1, UNIT, BLOCK), jnp.float32)
    operands = [own, other, left_root, root_own, root_other, left_in, right_in]
    return call(
        finish_body,
        "finish",
        scalars,
        (1,),
        [whole(o.shape) for o in operands],
        operands,
        [whole(result.shape)] * 3,
        [result] * 3,
        flops=20 * UNIT * BLOCK * BLOCK,
        scratch=[
            pltpu.VMEM((BLOCK, BLOCK), jnp.bfloat16),
            pltpu.VMEM((BLOCK, BLOCK), jnp.bfloat16),
            pltpu.VMEM((BLOCK, BLOCK), jnp.bfloat16),
        ],
    )


def per_device(
    inputs, cotangent, token_mask, block_owner, stat_left, stat_right, root_left, root_right
):
    own_group = lax.axis_index("grp")
    position = lax.axis_index("ctx")
    count = 4 * Z

    def to_core(value):
        return lax.ppermute(value, "ctx", [(i, i ^ 1) for i in range(count)])

    def over_y(value):
        return lax.ppermute(value, "ctx", [(i, i ^ 2) for i in range(count)])

    def along_z(value, swap=0):
        pairs = [(i, (i + (4 if i % 2 == 0 else -4)) % count ^ swap) for i in range(count)]
        return lax.ppermute(value, "ctx", pairs)

    scalars = jnp.stack(
        [own_group // (GROUPS // 2), position // 4, position % 2, position // 2 % 2]
    ).astype(jnp.int32)
    weights = cotangent, token_mask[None]
    root_other = to_core(root_right[0])
    parts, arrived, crossed = {}, {}, {}
    last = []
    for token in ORDER:
        name, steps = token[0], token[1:]
        if name == "m":
            distance = int(steps)
            if distance == 3:
                last.append(root_other)
            keep, sent, *more = multiply(scalars, weights, inputs, distance, last)
            if more:
                weights = more[0]
            last = [keep]
            parts[distance] = keep, to_core(sent)
        elif steps[0] == "x":
            sent, own = cross(token, scalars, parts[0], arrived["a"], last)
            last = [own]
            crossed["a"] = own, over_y(sent)
        elif name == "y":
            distances = [int(step) for step in steps]
            sent = across(token, scalars, [parts[distance] for distance in distances], last)
            last = [sent]
            sent, start = over_y(sent), 0
            for distance in distances:
                lanes = parts[distance][0].shape[1] // 2
                shape, index = (HALF + TAIL, lanes), start // lanes
                crossed[distance] = sent, pl.BlockSpec(shape, lambda i, s, index=index: (0, index))
                start += lanes
        else:
            distance = int(steps)
            lanes = parts[distance][0].shape[1]
            outs = 2 if distance == 1 else 1
            adds = [(value, whole(value.shape)) for value in arrived.get(name, [])]
            place = first_place
            if name == "b":
                lanes //= 2
                place = own_place
                adds.insert(0, crossed[distance])
            half = 0 if name == "a" else 1
            made = hop(token, scalars, parts[distance], half, lanes, place, adds, outs, last)
            last = [made[-1]]
            arrived[name] = [along_z(value, swap) for swap, value in enumerate(made)]
    block = collect(scalars, *crossed["a"], parts[0], [crossed[0][0]] + arrived["b"])

    rotation = lax.dynamic_index_in_dim(block_owner[:, 0], position // 2, 0, keepdims=False)

    def rotated(steps):
        if steps == 0:
            return lambda value: value
        pairs = [(source, (source + steps) % GROUPS) for source in range(GROUPS)]
        return lambda value: lax.ppermute(value, "grp", pairs)

    block = lax.switch(rotation, [rotated(steps) for steps in range(GROUPS)], block)
    return tuple(
        finish(
            scalars, block, to_core(block), root_left, root_right, root_other, stat_left, stat_right
        )
    )


def solution(mesh):
    in_specs = (
        P(None, "ctx", None),
        P("ctx", "grp"),
        P("ctx"),
        P(),
        P("grp", "ctx", None),
        P("grp", "ctx", None),
        P("grp", "ctx", None),
        P("grp", "ctx", None),
    )
    out_specs = (P("grp", "ctx", None), P("grp", "ctx", None), P("grp", "ctx", None))
    return jax.shard_map(
        per_device, mesh=mesh, in_specs=in_specs, out_specs=out_specs, check_vma=False
    )
```

```python
import functools

import jax
import jax.numpy as jnp
from jax import lax
from jax.experimental import pallas as pl
from jax.experimental.pallas import tpu as pltpu
from jax.sharding import PartitionSpec as P

decay_rate = 0.95
Z = 8
GROUPS = 8
UNIT = 256
BLOCK = 512
TAIL = 16
LEVELS = 32760.0
SMALLEST = 2.0**-100
MIB = 1 << 20
HALF = UNIT
LANES = 4 * UNIT
ORDER = ("m4", "m3", "a4", "m2", "y34", "a3", "m1", "m0", "b4", "a2", "y2", "b3", "y1", "a1", "b2", "y0", "ax", "b1")
COSTS = {4: 10000000000, 3: 20000000000, 2: 20000000000, 1: 20000000000, 0: 10000000000}
HOP_COST = 3000000000


def rows_tile(rows):
    shape = (TAIL, rows[0].shape[1])
    line = lax.broadcasted_iota(jnp.int32, shape, 0)
    tile = jnp.zeros(shape, jnp.float32)
    for i, row in enumerate(rows):
        tile = jnp.where(line == i, row, tile)
    return tile.astype(jnp.int32).astype(jnp.int16)


def coded(value):
    top = jnp.maximum(jnp.max(jnp.abs(value), axis=0, keepdims=True), SMALLEST)
    code = jnp.ceil(jnp.log2(top) * 256.0)
    inverse = LEVELS / jnp.exp2(code * (1.0 / 256.0))
    return jnp.round(value * inverse).astype(jnp.int32).astype(jnp.int16), code


def scales(tile):
    code = tile.astype(jnp.int32).astype(jnp.float32)
    return jnp.exp2(code * (1.0 / 256.0)) * (1.0 / LEVELS)


def decoded(data, scale):
    return data.astype(jnp.int32).astype(jnp.float32) * scale


def message(value):
    data, code = coded(value)
    return jnp.concatenate([data, rows_tile([code])], 0)


def opened(value):
    return decoded(value[:HALF], scales(value[HALF:])[0:1])


def whole(shape):
    return pl.BlockSpec(shape, lambda *a: (0,) * len(shape))


def wire(lanes):
    return jax.ShapeDtypeStruct((HALF + TAIL, lanes), jnp.int16)


def plain(lanes):
    return jax.ShapeDtypeStruct((HALF, lanes), jnp.float32)


def call(body, name, scalars, grid, in_specs, operands, out_specs, out_shape, after=(), moved=1024, flops=HOP_COST, scratch=(), vmem=24):
    count = len(operands)

    def ordered(scalar_refs, *refs):
        body(scalar_refs, *refs[:count], *refs[count + len(after) :])

    return pl.pallas_call(
        ordered,
        name=name,
        grid_spec=pltpu.PrefetchScalarGridSpec(
            num_scalar_prefetch=1,
            grid=grid,
            in_specs=list(in_specs) + [pl.BlockSpec(memory_space=pl.ANY)] * len(after),
            out_specs=out_specs,
            scratch_shapes=list(scratch),
        ),
        out_shape=out_shape,
        compiler_params=pltpu.CompilerParams(vmem_limit_bytes=vmem * MIB),
        cost_estimate=pl.CostEstimate(flops=flops, bytes_accessed=moved, transcendentals=0),
    )(scalars, *operands, *after)


def pick(condition, first, second):
    return jnp.where(condition, first, second), jnp.where(condition, second, first)


def by_core(left, right, is_first):
    lower = jnp.concatenate([left[:, :UNIT], right[:, :UNIT]], 1)
    upper = jnp.concatenate([left[:, UNIT:], right[:, UNIT:]], 1)
    return pick(is_first, lower, upper)


def multiply_body(scalars, weights, sent_in, kept_in, keep_ref, sent_ref):
    contract = ((0,), (0,))
    partial = product(weights[...], sent_in[0], contract)
    for half in range(2):
        sent_ref[half] = message(partial[half * HALF : (half + 1) * HALF])
    keep_ref[...] = product(weights[...], kept_in[0], contract)


def end_body(scalars, weights, *refs, masking):
    if masking:
        mask_ref, left_in, right_in, keep_ref, sent_ref, masked_ref = refs
        rows = jnp.broadcast_to(mask_ref[...].astype(jnp.float32), (8, mask_ref.shape[1]))
        column = rows.T[:, 0:1].astype(jnp.bfloat16)
        masked_ref[...] = weights[...] * column
        weights = masked_ref
    else:
        left_in, right_in, keep_ref, sent_ref = refs
    contract = ((0,), (0,))
    left = product(weights[...], left_in[0], contract)
    right = product(weights[...], right_in[0], contract)
    is_first = scalars[2] == 0
    if masking:
        kept, sent = pick(is_first, left[:HALF], right[:HALF])
    else:
        kept, sent = by_core(left[:HALF], right[:HALF], is_first)
    keep_ref[:HALF] = kept
    sent_ref[0] = message(sent)
    kept, sent = by_core(left[HALF:], right[HALF:], is_first)
    keep_ref[HALF:] = kept
    sent_ref[1] = message(sent)


def multiply(scalars, weights, inputs, distance, after):
    tokens = inputs.shape[1]
    width = BLOCK
    at_end = distance in (0, Z // 2)

    def spec(way):
        def index(j, s):
            if at_end:
                return s[0], 0, (s[1] + distance) % Z * 2 + way
            sign = 2 * way - 1
            target = (s[1] + sign * (1 - 2 * s[2]) * distance + Z) % Z
            return s[0], 0, target * 2 + j

        return pl.BlockSpec((1, tokens, width), index)

    lanes = LANES // 2 if at_end else LANES
    masking = distance == Z // 2
    body = functools.partial(end_body, masking=masking) if at_end else multiply_body
    first = list(weights) if masking else [weights]
    more = [jax.ShapeDtypeStruct((tokens, BLOCK), jnp.bfloat16)] if masking else []
    return call(
        body,
        "multiply",
        scalars,
        (lanes // width,),
        [whole(o.shape) for o in first] + [spec(0), spec(1)],
        first + [inputs, inputs],
        [
            pl.BlockSpec((BLOCK, width), lambda j, s: (0, j)),
            pl.BlockSpec((2, HALF + TAIL, width), lambda j, s: (0, 0, j)),
        ]
        + [whole(o.shape) for o in more],
        [
            jax.ShapeDtypeStruct((BLOCK, lanes), jnp.float32),
            jax.ShapeDtypeStruct((2, HALF + TAIL, lanes), jnp.int16),
        ]
        + more,
        after=after,
        flops=COSTS[distance],
        vmem=24,
    )


def part_specs(half, lanes, place):
    return [
        pl.BlockSpec((HALF, lanes), lambda i, s: (half, place(s))),
        pl.BlockSpec((1, HALF + TAIL, lanes), lambda i, s: (half, 0, place(s))),
    ]


def first_place(s):
    return 0


def own_place(s):
    return s[3]


def other_place(s):
    return 1 - s[3]


def hop_body(scalars, keep, got, *refs, count, outs):
    value = keep[...] + opened(got[0])
    for ref in refs[:count]:
        more = opened(ref[...])
        if more.shape[1] < value.shape[1]:
            nothing = jnp.zeros_like(more)
            lower, upper = jnp.concatenate([more, nothing], 1), jnp.concatenate([nothing, more], 1)
            more = jnp.where(scalars[2] == 0, lower, upper)
        value = value + more
    if outs == 1:
        refs[-1][...] = message(value)
        return
    is_first = scalars[2] == 0
    half = value.shape[1] // 2
    if half == UNIT:
        own, other = pick(is_first, value[:, :UNIT], value[:, UNIT:])
    else:
        own, other = by_core(value[:, :half], value[:, half:], is_first)
    refs[-2][...] = message(own)
    refs[-1][...] = message(other)


def hop(name, scalars, part, half, lanes, place, adds, outs, after):
    keep, got = part
    shape = wire(lanes // outs)
    return call(
        functools.partial(hop_body, count=len(adds), outs=outs),
        name,
        scalars,
        (1,),
        part_specs(half, lanes, place) + [spec for _, spec in adds],
        [keep, got] + [value for value, _ in adds],
        [whole(shape.shape)] * outs,
        [shape] * outs,
        after=after,
    )


def across_body(scalars, *refs):
    out, start = refs[-1], 0
    for keep, got in zip(refs[:-1:2], refs[1:-1:2]):
        value = keep[...] + opened(got[0])
        lanes = value.shape[1]
        out[:, start : start + lanes] = message(value)
        start += lanes


def across(name, scalars, chosen, after):
    specs, operands, total = [], [], 0
    for keep, got in chosen:
        lanes = keep.shape[1] // 2
        specs += part_specs(1, lanes, other_place)
        operands += [keep, got]
        total += lanes
    shape = wire(total)
    return call(
        across_body,
        name,
        scalars,
        (1,),
        specs,
        operands,
        [whole(shape.shape)],
        [shape],
        after=after,
    )[0]


def cross_body(scalars, keep, got, up, down, sent, kept):
    value = keep[...] + opened(got[0]) + opened(up[...]) + opened(down[...])
    kept[...], other = pick(scalars[3] == 0, value[:, :UNIT], value[:, UNIT:])
    sent[...] = message(other)


def cross(name, scalars, part, adds, after):
    keep, got = part
    return call(
        cross_body,
        name,
        scalars,
        (1,),
        part_specs(0, 2 * UNIT, first_place) + [whole(o.shape) for o in adds],
        [keep, got] + adds,
        [whole(wire(UNIT).shape), whole((HALF, UNIT))],
        [wire(UNIT), plain(UNIT)],
        after=after,
    )


def collect_body(scalars, own, over, keep, got, crossed, up, down, out):
    first, first_code = coded(own[...] + opened(over[...]))
    value = keep[...] + opened(got[0]) + opened(crossed[...])
    second, second_code = coded(value + opened(up[...]) + opened(down[...]))
    out[0:UNIT, :] = first
    out[UNIT:BLOCK, :] = second
    out[BLOCK : BLOCK + TAIL, :] = rows_tile([first_code, second_code])


def collect(scalars, own, over, part, adds):
    shape = (BLOCK + TAIL, UNIT)
    keep, got = part
    return call(
        collect_body,
        "collect",
        scalars,
        (1,),
        [whole(own.shape), whole(over.shape)]
        + part_specs(1, UNIT, own_place)
        + [whole(o.shape) for o in adds],
        [own, over, keep, got] + adds,
        [whole(shape)],
        [jax.ShapeDtypeStruct(shape, jnp.int16)],
    )[0]


def read_block(ref):
    scale = scales(ref[BLOCK : BLOCK + TAIL, :])
    return jnp.concatenate(
        [decoded(ref[0:UNIT, :], scale[0:1]), decoded(ref[UNIT:BLOCK, :], scale[1:2])], 0
    )


def product(a, b, contract):
    return lax.dot_general(a, b, (contract, ((), ())), preferred_element_type=jnp.float32)


def split(value):
    high = value.astype(jnp.bfloat16)
    return high, (value - high.astype(jnp.float32)).astype(jnp.bfloat16)


BY_ROWS = ((0,), (0,))
BY_COLUMNS = ((1,), (1,))


def three(a_high, a_low, b_high, b_low, contract):
    term = product(a_high, b_high, contract)
    return term + product(a_high, b_low, contract) + product(a_low, b_high, contract)


def begin_body(scalars, own_ref, left_root, high, low, left_part, right_part, applied_part):
    start = pl.multiple_of(scalars[2] * UNIT, UNIT)
    here = pl.ds(start, UNIT)
    own_high, own_low = split(read_block(own_ref))
    high[...] = own_high
    low[...] = own_low
    left_part[...] = three(own_high, own_low, own_high, own_low, BY_ROWS)
    right_part[...] = three(high[here, :], low[here, :], own_high, own_low, BY_COLUMNS)
    root = left_root[0, :, here]
    applied_part[...] = product(root, own_high, BY_COLUMNS) + product(root, own_low, BY_COLUMNS)


def finish_body(
    scalars, other_ref, own_high, own_low, left_part, right_part, applied_part, left_root,
    root_own, root_other, left_in, right_in, left_out, right_out, update_out, high, low, root,
):
    core = scalars[2]
    other_high, other_low = split(read_block(other_ref))
    high[...] = other_high
    low[...] = other_low
    rate = 1.0 - decay_rate
    cross_term = three(own_high[...], own_low[...], other_high, other_low, BY_ROWS)
    for c in range(2):
        mine, theirs = pl.ds(c * UNIT, UNIT), pl.ds((1 - c) * UNIT, UNIT)

        @pl.when(core == c)
        def _():
            left_out[0, :, mine] = decay_rate * left_in[0, :, mine] + rate * left_part[...]
            left_out[0, :, theirs] = decay_rate * left_in[0, :, theirs] + rate * cross_term
            root[mine, :] = root_own[0]
            root[theirs, :] = root_other[...]

    here = pl.ds(pl.multiple_of(core * UNIT, UNIT), UNIT)
    there = pl.ds(pl.multiple_of((1 - core) * UNIT, UNIT), UNIT)
    term = right_part[...] + three(high[here, :], low[here, :], other_high, other_low, BY_COLUMNS)
    right_out[0] = decay_rate * right_in[0] + rate * term
    left = left_root[0, :, there]
    applied = applied_part[...] + product(left, other_high, BY_COLUMNS)
    applied_high, applied_low = split(applied + product(left, other_low, BY_COLUMNS))
    straight = ((1,), (0,))
    update_out[0] = product(applied_high, root[...], straight) + product(
        applied_low, root[...], straight
    )


def finish(scalars, own, other, left_root, root_own, root_other, left_in, right_in):
    result = jax.ShapeDtypeStruct((1, UNIT, BLOCK), jnp.float32)
    half = jax.ShapeDtypeStruct((BLOCK, UNIT), jnp.bfloat16)
    shapes = [half, half] + [jax.ShapeDtypeStruct((UNIT, n), jnp.float32) for n in (UNIT, BLOCK, BLOCK)]
    begun = call(
        begin_body,
        "begin",
        scalars,
        (1,),
        [whole(own.shape), whole(left_root.shape)],
        [own, left_root],
        [whole(o.shape) for o in shapes],
        shapes,
    )
    operands = [other, *begun, left_root, root_own, root_other, left_in, right_in]
    return call(
        finish_body,
        "finish",
        scalars,
        (1,),
        [whole(o.shape) for o in operands],
        operands,
        [whole(result.shape)] * 3,
        [result] * 3,
        scratch=[
            pltpu.VMEM((BLOCK, UNIT), jnp.bfloat16),
            pltpu.VMEM((BLOCK, UNIT), jnp.bfloat16),
            pltpu.VMEM((BLOCK, BLOCK), jnp.bfloat16),
        ],
    )


def per_device(
    inputs, cotangent, token_mask, block_owner, stat_left, stat_right, root_left, root_right
):
    own_group = lax.axis_index("grp")
    position = lax.axis_index("ctx")
    count = 4 * Z

    def to_core(value):
        return lax.ppermute(value, "ctx", [(i, i ^ 1) for i in range(count)])

    def over_y(value):
        return lax.ppermute(value, "ctx", [(i, i ^ 2) for i in range(count)])

    def along_z(value, swap=0):
        pairs = [(i, (i + (4 if i % 2 == 0 else -4)) % count ^ swap) for i in range(count)]
        return lax.ppermute(value, "ctx", pairs)

    scalars = jnp.stack(
        [own_group // (GROUPS // 2), position // 4, position % 2, position // 2 % 2]
    ).astype(jnp.int32)
    weights = cotangent, token_mask[None]
    root_other = to_core(root_right[0])
    parts, arrived, crossed = {}, {}, {}
    last = []
    for token in ORDER:
        name, steps = token[0], token[1:]
        if name == "m":
            distance = int(steps)
            if distance == 3:
                last.append(root_other)
            keep, sent, *more = multiply(scalars, weights, inputs, distance, last)
            if more:
                weights = more[0]
            last = [keep]
            parts[distance] = keep, to_core(sent)
        elif steps[0] == "x":
            sent, own = cross(token, scalars, parts[0], arrived["a"], last)
            last = [own]
            crossed["a"] = own, over_y(sent)
        elif name == "y":
            distances = [int(step) for step in steps]
            sent = across(token, scalars, [parts[distance] for distance in distances], last)
            last = [sent]
            sent, start = over_y(sent), 0
            for distance in distances:
                lanes = parts[distance][0].shape[1] // 2
                shape, index = (HALF + TAIL, lanes), start // lanes
                crossed[distance] = sent, pl.BlockSpec(shape, lambda i, s, index=index: (0, index))
                start += lanes
        else:
            distance = int(steps)
            lanes = parts[distance][0].shape[1]
            outs = 2 if distance == 1 else 1
            adds = [(value, whole(value.shape)) for value in arrived.get(name, [])]
            place = first_place
            if name == "b":
                lanes //= 2
                place = own_place
                adds.insert(0, crossed[distance])
            half = 0 if name == "a" else 1
            made = hop(token, scalars, parts[distance], half, lanes, place, adds, outs, last)
            last = [made[-1]]
            arrived[name] = [along_z(value, swap) for swap, value in enumerate(made)]
    block = collect(scalars, *crossed["a"], parts[0], [crossed[0][0]] + arrived["b"])

    rotation = lax.dynamic_index_in_dim(block_owner[:, 0], position // 2, 0, keepdims=False)

    def rotated(steps):
        if steps == 0:
            return lambda value: value
        pairs = [(source, (source + steps) % GROUPS) for source in range(GROUPS)]
        return lambda value: lax.ppermute(value, "grp", pairs)

    block = lax.switch(rotation, [rotated(steps) for steps in range(GROUPS)], block)
    return tuple(
        finish(
            scalars, block, to_core(block), root_left, root_right, root_other, stat_left, stat_right
        )
    )


def solution(mesh):
    in_specs = (
        P(None, "ctx", None),
        P("ctx", "grp"),
        P("ctx"),
        P(),
        P("grp", "ctx", None),
        P("grp", "ctx", None),
        P("grp", "ctx", None),
        P("grp", "ctx", None),
    )
    out_specs = (P("grp", "ctx", None), P("grp", "ctx", None), P("grp", "ctx", None))
    return jax.shard_map(
        per_device, mesh=mesh, in_specs=in_specs, out_specs=out_specs, check_vma=False
    )
```
